32 devices in a mesh: rows: 32 (over z, y, x, core).
Axes of the slice: x: 2, y: 2, z: 4, core: 2. Of those that a mesh axis runs over, the one named last changes fastest.
Arguments:
- points: float32 [8, 262144], P(None, 'rows'), may hold values from -6 to 6
- inv_scales: float32 [8], replicated, may hold values from 0.25 to 0.8
- pivots: int32 [3, 256], replicated, may hold values from 0 to 262143, as said below
Outputs:
- factor: float32 [262144, 768], P('rows')
- residual: float32 [262144], P('rows')
The draws below stay inside these ranges and needn't reach their ends.
Inputs may be any that keep to these rules, and one draw needn't show every extreme that they name: `pivots`: each entry is a point index (column of points); all 768 entries are distinct. In each panel at most 32 entries lie among one device's points (indices d * 8192 to (d + 1) * 8192 - 1), and in every panel some device holds exactly 32.
All inputs are finite; a program needn't handle non-finite values.
Results may differ from the reference program's by a relative error of at most 0.0003.
Values sent between devices are 32-bit elements; how exact they have to be, the bound alone decides.
No kernel may reach another device: no remote copies, remote signals or barrier semaphores. Data moves between devices by JAX's collectives and lax.ppermute only.
A program may use at most 192 MiB of HBM per device.

```python
import math
import jax
import jax.numpy as jnp
from jax import lax

DIM = 8
PANEL = 256
PANELS = 3
PTS_DEV = 8192
NPTS = 262144
PIV_MOST = 32


def draw_pivots(key, part):
    key = jax.random.fold_in(key, 11)
    device_count = NPTS // PTS_DEV
    key_rows, key_panels = jax.random.split(key, 2)
    row_order = jax.random.permutation(key_rows, PTS_DEV).astype(jnp.int32)
    position = jnp.arange(PANEL, dtype=jnp.int32)
    is_heavy = position < PIV_MOST
    others = position - PIV_MOST
    panel_rows = []
    for which_panel in range(PANELS):
        key_panel = jax.random.fold_in(key_panels, which_panel)
        key_owner, key_shuffle = jax.random.split(key_panel, 2)
        device_order = jax.random.permutation(key_owner, device_count).astype(jnp.int32)
        owner_place = jnp.where(is_heavy, 0, 1 + others % (device_count - 1))
        slot_rank = jnp.where(is_heavy, position, others // (device_count - 1))
        owners = device_order[owner_place]
        local_rows = row_order[which_panel * PIV_MOST + slot_rank]
        indices = owners * PTS_DEV + local_rows
        shuffle = jax.random.permutation(key_shuffle, PANEL)
        panel_rows.append(indices[shuffle].astype(jnp.int32))
    return jnp.stack(panel_rows, axis=0).astype(jnp.int32)


def shard_levels(key, extent, pieces, smallest, top_value):
    factor_of = 1.0
    for axis_at, shards_of in pieces:
        heights = jax.random.uniform(jax.random.fold_in(jax.random.fold_in(key, 6), axis_at), (shards_of,), jnp.float32, smallest / len(pieces), top_value / len(pieces))
        factor_of = factor_of * jnp.repeat(jnp.exp(heights), extent[axis_at] // shards_of).reshape((-1,) + (1,) * (len(extent) - 1 - axis_at))
    return factor_of


def bell_draw(stream_key, extent, scale, limit, cuts=(), kind=jnp.bfloat16):
    loudness = shard_levels(stream_key, extent, cuts, -0.22, 0.18) if cuts else 1.0
    drawn = jax.random.normal(stream_key, extent, jnp.float32) * scale * loudness
    return jnp.minimum(jnp.maximum(drawn, -limit), limit).astype(kind)


def setup_inputs(seed: int = 0) -> dict:
    key_of = jax.random.split(jax.random.key(seed), 4)
    points = bell_draw(key_of[0], (DIM, NPTS), 1.0, 6.0, ((1, 32),), jnp.float32)
    inv_scales = jnp.clip(jnp.exp(jax.random.uniform(key_of[1], (DIM,), jnp.float32, math.log(0.25), math.log(0.8))), 0.25, 0.8)
    pivots = draw_pivots(jax.random.fold_in(key_of[3], 71), 0)
    return dict(points=points, inv_scales=inv_scales, pivots=pivots)


nugget = 0.1

def kernel_tile(left_pts, right_pts, scales):
    left_scaled = left_pts * scales[:, None]
    right_scaled = right_pts * scales[:, None]
    inner_prod = lax.dot_general(left_scaled.astype(jnp.float32), right_scaled.astype(jnp.float32), (((0,), (0,)), ((), ())), precision=lax.Precision.HIGHEST, preferred_element_type=jnp.float32)
    squared = jnp.sum(left_scaled * left_scaled, axis=0)[:, None] + jnp.sum(right_scaled * right_scaled, axis=0)[None, :] - 2.0 * inner_prod
    return jnp.exp(-0.5 * squared)

def reference(points, inv_scales, pivots):
    block_count = NPTS // PTS_DEV
    point_blocks = points.reshape(DIM, block_count, PTS_DEV).transpose(1, 0, 2)
    residual = jnp.ones((NPTS,), jnp.float32)
    identity = jnp.eye(PANEL, dtype=jnp.float32)
    factor_parts = []
    for which_panel in range(PANELS):
        pivot_index = pivots[which_panel]
        piv_points = points[:, pivot_index]
        pivot_block = kernel_tile(piv_points, piv_points, inv_scales)
        if factor_parts:
            piv_factor = jnp.concatenate([part[pivot_index] for part in factor_parts], axis=1)
            pivot_block = pivot_block - jnp.dot(piv_factor.astype(jnp.float32), piv_factor.T.astype(jnp.float32), precision=lax.Precision.HIGHEST, preferred_element_type=jnp.float32)
        pivot_block = pivot_block + nugget * identity
        lower_factor = jnp.linalg.cholesky(pivot_block)
        inverse = jax.scipy.linalg.solve_triangular(lower_factor, identity, lower=True)
        if factor_parts:
            part_blocks = tuple((part.reshape(block_count, PTS_DEV, PANEL) for part in factor_parts))

            def one_block(items):
                kernel_cols = kernel_tile(items[0], piv_points, inv_scales)
                earlier = jnp.concatenate(items[1], axis=1)
                kernel_cols = kernel_cols - jnp.dot(earlier.astype(jnp.float32), piv_factor.T.astype(jnp.float32), precision=lax.Precision.HIGHEST, preferred_element_type=jnp.float32)
                return jnp.dot(kernel_cols.astype(jnp.float32), inverse.T.astype(jnp.float32), precision=lax.Precision.HIGHEST, preferred_element_type=jnp.float32)
            new_columns = lax.map(one_block, (point_blocks, part_blocks))
        else:

            def first_block(block_pts):
                kernel_cols = kernel_tile(block_pts, piv_points, inv_scales)
                return jnp.dot(kernel_cols.astype(jnp.float32), inverse.T.astype(jnp.float32), precision=lax.Precision.HIGHEST, preferred_element_type=jnp.float32)
            new_columns = lax.map(first_block, point_blocks)
        new_columns = new_columns.reshape(NPTS, PANEL)
        residual = residual - jnp.sum(new_columns * new_columns, axis=1)
        factor_parts.append(new_columns)
    return (jnp.concatenate(factor_parts, axis=1), residual)
```

```python
import functools

import jax
import jax.numpy as jnp
from jax import lax
from jax.experimental import pallas as pl
from jax.experimental.pallas import tpu as pltpu
from jax.sharding import PartitionSpec as P

nugget = 0.1
exp2_scale = 1.2011224087864498
group = 8
lanes = 128
block = 128
feature_rows = 64
high = lax.Precision.HIGHEST


def product(a, b, a_dim=1, b_dim=0, precision=None):
    return lax.dot_general(
        a,
        b,
        (((a_dim,), (b_dim,)), ((), ())),
        precision=precision,
        preferred_element_type=jnp.float32,
    )


def iota(shape, dim):
    return lax.broadcasted_iota(jnp.int32, shape, dim)


def widen(x):
    return x.astype(jnp.float32)


def narrow(x):
    return x.astype(jnp.bfloat16)


def select_kernel(row_count, slot_count, device_count, points_ref, pivots_ref, send_ref, place_ref):
    panels, pivot_count = pivots_ref.shape
    me = lax.axis_index("rows")
    before = narrow(
        jnp.where(iota((pivot_count, pivot_count), 0) < iota((pivot_count, pivot_count), 1), 1.0, 0.0)
    )
    chosen_parts = []
    value_parts = []
    for panel in range(panels):
        index = pivots_ref[panel : panel + 1, :]
        owner = lax.div(index, row_count)
        local = index - owner * row_count
        owned = jnp.where(
            iota((device_count, pivot_count), 0) == jnp.broadcast_to(owner, (device_count, pivot_count)), 1.0, 0.0
        )
        counts = product(narrow(owned), before)
        rank = jnp.sum(owned * counts, axis=0, keepdims=True).astype(jnp.int32)
        slot = rank + panel * slot_count
        place_ref[panel : panel + 1, :] = owner * lanes + slot
        mine = jnp.where(owner == me, slot, -1)
        chosen_parts.append(
            jnp.where(iota((lanes, pivot_count), 0) == jnp.broadcast_to(mine, (lanes, pivot_count)), 1.0, 0.0)
        )
        tile = lax.div(local, lanes)
        lane = local - tile * lanes
        which = iota((group, pivot_count), 0)
        value_parts.append(
            jnp.where(which == 0, widen(tile), jnp.where(which == 1, widen(lane), 0.0))
        )
    chosen = narrow(jnp.concatenate(chosen_parts, axis=1))
    values = narrow(jnp.concatenate(value_parts, axis=1))
    found = product(values, chosen, 1, 1).astype(jnp.int32)
    tile = jnp.broadcast_to(found[0:1, :], (group, lanes))
    lane = jnp.broadcast_to(found[1:2, :], (group, lanes))
    taken = jnp.zeros((group, lanes), jnp.float32)
    for t in range(row_count // lanes):
        here = jnp.take_along_axis(points_ref[:, t * lanes : (t + 1) * lanes], lane, axis=1)
        taken = jnp.where(tile == t, here, taken)
    for d in range(device_count):
        send_ref[d] = taken


def scale_column(scales_ref):
    sub = iota((group, 1), 0)
    column = jnp.zeros((group, 1), jnp.float32)
    for d in range(group):
        column = jnp.where(sub == d, scales_ref[d], column)
    return column * exp2_scale


def split3(x):
    top = widen(narrow(x))
    rest = x - top
    mid = widen(narrow(rest))
    return top, mid, widen(narrow(rest - mid))


def features(scaled, left):
    top, mid, low = split3(scaled)
    count = scaled.shape[1]
    norm = split3(jnp.broadcast_to(-0.5 * jnp.sum(scaled * scaled, axis=0, keepdims=True), (group, count)))
    sub = iota((group, count), 0)
    at = 0 if left else 3
    extra = jnp.where(sub < 6, 1.0, 0.0)
    for i in range(3):
        extra = jnp.where(sub == at + i, norm[i], extra)
    zero = jnp.zeros((group, count), jnp.float32)
    if left:
        parts = [top, top, mid, top, low, mid, extra, zero]
    else:
        parts = [top, mid, top, low, top, mid, extra, zero]
    return jnp.concatenate(parts, axis=0)


def factor_block(matrix):
    groups = block // group
    sub = iota((group, block), 0)
    lane = iota((group, block), 1)
    rows = [matrix[g * group : (g + 1) * group, :] for g in range(groups)]
    inv = [jnp.where(lane == sub + g * group, 1.0, 0.0) for g in range(groups)]
    done = []

    def spread(row, at):
        return jnp.broadcast_to(row[at : at + 1, :], (group, block))

    for w in range(groups):
        cols = [
            [
                jnp.broadcast_to(rows[g][:, w * group + k : w * group + k + 1], (group, block))
                for k in range(group)
            ]
            for g in range(w, groups)
        ]
        near = list(cols[0])
        row_s, row_x, forward = rows[w], inv[w], inv[w]
        diag = None
        for j in range(group):
            pivot = spread(near[j], j)
            recip = 1.0 / pivot
            mult = near[j] * recip
            both = jnp.where(sub == j, 1.0 - recip, mult)
            below = jnp.where(sub > j, mult, 0.0)
            diag = pivot if diag is None else jnp.where(sub >= j, pivot, diag)
            row_s = row_s - both * spread(row_s, j)
            row_x = row_x - both * spread(row_x, j)
            if j < group - 1:
                forward = forward - below * spread(forward, j)
            for k in range(j + 1, group):
                near[k] = near[k] - both * spread(near[k], j)
        done.append(forward * lax.rsqrt(diag))
        for g in range(w + 1, groups):
            c = cols[g - w]
            s, x = rows[g], inv[g]
            for k in range(group):
                s = s - c[k] * spread(row_s, k)
                x = x - c[k] * spread(row_x, k)
            rows[g], inv[g] = s, x
    return jnp.concatenate(done, axis=0)


def invert_factor(s_ref, w_ref, blocks):
    at = lambda i: slice(i * block, (i + 1) * block)
    total = blocks * block
    for b in range(blocks):
        x = factor_block(s_ref[at(b), at(b)])
        w_ref[at(b), at(b)] = x
        if b > 0:
            w_ref[at(b), 0 : b * block] = product(x, w_ref[at(b), 0 : b * block], precision=high)
        if b + 1 < blocks:
            w_ref[at(b), (b + 1) * block : total] = jnp.zeros((block, total - (b + 1) * block), jnp.float32)
            y = product(x, s_ref[at(b), (b + 1) * block : total], precision=high)
            for i in range(b + 1, blocks):
                mine = y[:, (i - b - 1) * block : (i - b) * block]
                s_ref[at(i), i * block : total] = s_ref[at(i), i * block : total] - product(
                    mine, y[:, (i - b - 1) * block :], 0, 0, high
                )
            for i in range(b + 1, blocks):
                mine = y[:, (i - b - 1) * block : (i - b) * block]
                t = product(mine, w_ref[at(b), 0 : (b + 1) * block], 0, 0, high)
                if b > 0:
                    w_ref[at(i), 0 : b * block] = w_ref[at(i), 0 : b * block] - t[:, 0 : b * block]
                w_ref[at(i), at(b)] = -t[:, b * block :]


def pivot_kernel(
    device_count, place_ref, got_ref, scales_ref, right_ref, top_ref, low_ref, mean_ref, shift_ref, s_ref, w_ref
):
    panels, pivot_count = place_ref.shape
    total = panels * pivot_count
    parts = []
    for panel in range(panels):
        for half in range(pivot_count // lanes):
            place = place_ref[panel : panel + 1, half * lanes : (half + 1) * lanes]
            owner = jnp.broadcast_to(lax.div(place, lanes), (group, lanes))
            lane = jnp.broadcast_to(place, (group, lanes)) - owner * lanes
            taken = jnp.zeros((group, lanes), jnp.float32)
            for d in range(device_count):
                taken = jnp.where(owner == d, jnp.take_along_axis(got_ref[d], lane, axis=1), taken)
            parts.append(taken)
    scaled = jnp.concatenate(parts, axis=1) * scale_column(scales_ref)
    left = narrow(features(scaled, True))
    right = narrow(features(scaled, False))
    right_ref[...] = right
    kernel = jnp.exp2(product(left, right, 0, 0))
    mean = jnp.sum(kernel, axis=0, keepdims=True) * (1.0 / total)
    mean_ref[...] = jnp.broadcast_to(mean, (group, total))
    s_ref[...] = jnp.where(iota((total, total), 0) == iota((total, total), 1), kernel + nugget, kernel)
    invert_factor(s_ref, w_ref, total // block)
    inverse = w_ref[...]
    top = narrow(inverse)
    top_ref[...] = top
    low_ref[...] = narrow(inverse - widen(top))
    shift_ref[...] = product(jnp.broadcast_to(mean, (group, total)), inverse, 1, 1, high)


def rows_kernel(panel_width, points_ref, scales_ref, right_ref, top_ref, low_ref, mean_ref, shift_ref, out_ref, res_ref):
    total = right_ref.shape[1]
    scaled = points_ref[...] * scale_column(scales_ref)
    left = narrow(features(scaled, True))
    kernel = jnp.exp2(product(left, right_ref[...], 0, 0)) - mean_ref[0:1, :]
    top = narrow(kernel)
    low = narrow(kernel - widen(top))
    squares = None
    for p in range(total // panel_width):
        at = slice(p * panel_width, (p + 1) * panel_width)
        depth = (p + 1) * panel_width
        a = jnp.concatenate([top[:, :depth], low[:, :depth], top[:, :depth]], axis=1)
        b = jnp.concatenate([top_ref[at, :depth], top_ref[at, :depth], low_ref[at, :depth]], axis=1)
        new = product(a, b, 1, 1) + shift_ref[0:1, at]
        out_ref[:, at] = new
        for q in range(panel_width // lanes):
            piece = new[:, q * lanes : (q + 1) * lanes]
            squares = piece * piece if squares is None else squares + piece * piece
    res_ref[...] = 1.0 - jnp.sum(squares.T, axis=0, keepdims=True)


def on_device(points, inv_scales, pivots):
    dim, row_count = points.shape
    panels, pivot_count = pivots.shape
    device_count = lax.axis_size("rows")
    slot_count = 4 * pivot_count // device_count
    total = panels * pivot_count
    assert dim == group and panels * slot_count <= lanes
    f32, bf16 = jnp.float32, jnp.bfloat16
    shape = jax.ShapeDtypeStruct
    vmem = pl.BlockSpec(memory_space=pltpu.VMEM)
    smem = pl.BlockSpec(memory_space=pltpu.SMEM)
    params = pltpu.CompilerParams(vmem_limit_bytes=48 * 2**20)

    send, place = pl.pallas_call(
        functools.partial(select_kernel, row_count, slot_count, device_count),
        out_shape=(shape((device_count, group, lanes), f32), shape((panels, pivot_count), jnp.int32)),
        in_specs=[vmem, vmem],
        out_specs=(vmem, vmem),
        compiler_params=params,
        name="select",
    )(points, pivots)
    got = lax.all_to_all(send, "rows", 0, 0)
    right, top, low, mean, shift = pl.pallas_call(
        functools.partial(pivot_kernel, device_count),
        out_shape=(
            shape((feature_rows, total), bf16),
            shape((total, total), bf16),
            shape((total, total), bf16),
            shape((group, total), f32),
            shape((group, total), f32),
        ),
        in_specs=[vmem, vmem, smem],
        out_specs=(vmem,) * 5,
        scratch_shapes=[pltpu.VMEM((total, total), f32), pltpu.VMEM((total, total), f32)],
        compiler_params=params,
        name="pivots",
    )(place, got, inv_scales)
    tile = 512
    whole = lambda s: pl.BlockSpec(s, lambda i: (0,) * len(s))
    factor, residual = pl.pallas_call(
        functools.partial(rows_kernel, pivot_count),
        grid=(row_count // tile,),
        out_shape=(shape((row_count, total), f32), shape((1, row_count), f32)),
        in_specs=[
            pl.BlockSpec((group, tile), lambda i: (0, i)),
            smem,
            whole((feature_rows, total)),
            whole((total, total)),
            whole((total, total)),
            whole((group, total)),
            whole((group, total)),
        ],
        out_specs=(pl.BlockSpec((tile, total), lambda i: (i, 0)), pl.BlockSpec((1, tile), lambda i: (0, i))),
        compiler_params=params,
        name="rows",
    )(points, inv_scales, right, top, low, mean, shift)
    return factor, residual.reshape(row_count)


def solution(mesh):
    return jax.shard_map(
        on_device,
        mesh=mesh,
        in_specs=(P(None, "rows"), P(), P()),
        out_specs=(P("rows", None), P("rows")),
        check_vma=False,
    )
```

```python
import functools

import jax
import jax.numpy as jnp
from jax import lax
from jax.experimental import pallas as pl
from jax.experimental.pallas import tpu as pltpu
from jax.sharding import PartitionSpec as P

nugget = 0.1
exp2_scale = 1.2011224087864498
group = 8
lanes = 128
block = 128
window = 16
feature_rows = 64
high = lax.Precision.HIGHEST


def product(a, b, a_dim=1, b_dim=0, precision=None):
    return lax.dot_general(
        a,
        b,
        (((a_dim,), (b_dim,)), ((), ())),
        precision=precision,
        preferred_element_type=jnp.float32,
    )


def iota(shape, dim):
    return lax.broadcasted_iota(jnp.int32, shape, dim)


def widen(x):
    return x.astype(jnp.float32)


def narrow(x):
    return x.astype(jnp.bfloat16)


def select_kernel(row_count, slot_count, device_count, points_ref, pivots_ref, send_ref, place_ref):
    panels, pivot_count = pivots_ref.shape
    me = lax.axis_index("rows")
    before = narrow(
        jnp.where(iota((pivot_count, pivot_count), 0) < iota((pivot_count, pivot_count), 1), 1.0, 0.0)
    )
    chosen_parts = []
    value_parts = []
    for panel in range(panels):
        index = pivots_ref[panel : panel + 1, :]
        owner = lax.div(index, row_count)
        local = index - owner * row_count
        owned = jnp.where(
            iota((device_count, pivot_count), 0) == jnp.broadcast_to(owner, (device_count, pivot_count)), 1.0, 0.0
        )
        counts = product(narrow(owned), before)
        rank = jnp.sum(owned * counts, axis=0, keepdims=True).astype(jnp.int32)
        slot = rank + panel * slot_count
        place_ref[panel : panel + 1, :] = owner * lanes + slot
        mine = jnp.where(owner == me, slot, -1)
        chosen_parts.append(
            jnp.where(iota((lanes, pivot_count), 0) == jnp.broadcast_to(mine, (lanes, pivot_count)), 1.0, 0.0)
        )
        tile = lax.div(local, lanes)
        lane = local - tile * lanes
        which = iota((group, pivot_count), 0)
        value_parts.append(
            jnp.where(which == 0, widen(tile), jnp.where(which == 1, widen(lane), 0.0))
        )
    chosen = narrow(jnp.concatenate(chosen_parts, axis=1))
    values = narrow(jnp.concatenate(value_parts, axis=1))
    found = product(values, chosen, 1, 1).astype(jnp.int32)
    tile = jnp.broadcast_to(found[0:1, :], (group, lanes))
    lane = jnp.broadcast_to(found[1:2, :], (group, lanes))
    taken = jnp.zeros((group, lanes), jnp.float32)
    for t in range(row_count // lanes):
        here = jnp.take_along_axis(points_ref[:, t * lanes : (t + 1) * lanes], lane, axis=1)
        taken = jnp.where(tile == t, here, taken)
    for d in range(device_count):
        send_ref[d] = taken


def scale_column(scales_ref):
    sub = iota((group, 1), 0)
    column = jnp.zeros((group, 1), jnp.float32)
    for d in range(group):
        column = jnp.where(sub == d, scales_ref[d], column)
    return column * exp2_scale


def split3(x):
    top = widen(narrow(x))
    rest = x - top
    mid = widen(narrow(rest))
    return top, mid, widen(narrow(rest - mid))


def features(scaled, left):
    top, mid, low = split3(scaled)
    count = scaled.shape[1]
    norm = split3(jnp.broadcast_to(-0.5 * jnp.sum(scaled * scaled, axis=0, keepdims=True), (group, count)))
    sub = iota((group, count), 0)
    at = 0 if left else 3
    extra = jnp.where(sub < 6, 1.0, 0.0)
    for i in range(3):
        extra = jnp.where(sub == at + i, norm[i], extra)
    zero = jnp.zeros((group, count), jnp.float32)
    if left:
        parts = [top, top, mid, top, low, mid, extra, zero]
    else:
        parts = [top, mid, top, low, top, mid, extra, zero]
    return jnp.concatenate(parts, axis=0)


def spread(row, at):
    return jnp.broadcast_to(row[at : at + 1, :], row.shape)


def column(rows, at):
    return jnp.broadcast_to(rows[:, at : at + 1], rows.shape)


def tree_sum(terms):
    while len(terms) > 1:
        terms = [sum(terms[i : i + 2][1:], terms[i]) for i in range(0, len(terms), 2)]
    return terms[0]


def stack_left(x):
    top, mid, low = split3(x)
    return jnp.concatenate([top, top, mid, top, low, mid], axis=0)


def stack_right(x):
    top, mid, low = split3(x)
    return narrow(jnp.concatenate([top, mid, top, low, top, mid], axis=0))


def factor_block(matrix, answer):
    windows = block // window
    sub = iota((window, block), 0)
    lane = iota((window, block), 1)
    rows = [matrix[w * window : (w + 1) * window, :] for w in range(windows)]
    inv = [jnp.where(lane == sub + w * window, 1.0, 0.0) for w in range(windows)]
    for w in range(windows):
        first = w * window
        near = [column(rows[w], first + k) for k in range(window)]
        after = [column(rows[w + 1], first + k) for k in range(window)] if w + 1 < windows else []
        if w + 2 < windows:
            left = narrow(stack_left(rows[w]).T)[(w + 2) * window :, :]
        row_s, row_x, forward = rows[w], inv[w], inv[w]
        diag = None
        for j in range(0, window, 2):
            a, b, c = spread(near[j], j), spread(near[j + 1], j), spread(near[j + 1], j + 1)
            recip = 1.0 / (a * c - b * b)
            n1 = near[j] - jnp.where(sub == j, 1.0, 0.0)
            n2 = near[j + 1] - jnp.where(sub == j + 1, 1.0, 0.0)
            m1 = (n1 * c - n2 * b) * recip
            m2 = (n2 * a - n1 * b) * recip
            for k in range(j + 2, window):
                near[k] = near[k] - (m1 * spread(near[k], j) + m2 * spread(near[k], j + 1))
            over = 1.0 / a
            f1 = jnp.where(sub > j, near[j] * over, 0.0)
            f2 = jnp.where(sub > j + 1, (near[j + 1] - near[j] * (b * over)) * (a * recip), 0.0)
            diag = a if diag is None else jnp.where(sub >= j, a, diag)
            diag = jnp.where(sub >= j + 1, c - b * (b * over), diag)
            row_s = row_s - (m1 * spread(row_s, j) + m2 * spread(row_s, j + 1))
            row_x = row_x - (m1 * spread(row_x, j) + m2 * spread(row_x, j + 1))
            forward = forward - f1 * spread(forward, j)
            if j + 2 < window:
                forward = forward - f2 * spread(forward, j + 1)
        answer.append(forward * lax.rsqrt(diag))
        if w + 1 < windows:
            rows[w + 1] = rows[w + 1] - tree_sum([after[k] * spread(row_s, k) for k in range(window)])
            inv[w + 1] = inv[w + 1] - tree_sum([after[k] * spread(row_x, k) for k in range(window)])
        if w + 2 < windows:
            change = product(left, stack_right(jnp.concatenate([row_s, row_x], axis=1)))
            for v in range(w + 2, windows):
                at = (v - w - 2) * window
                rows[v] = rows[v] - change[at : at + window, :block]
                inv[v] = inv[v] - change[at : at + window, block:]
        yield w


def two_parts(x):
    top = narrow(x)
    return top, narrow(x - widen(top))


def gather_pivots(device_count, place_ref, got_ref):
    panels, pivot_count = place_ref.shape
    parts = []
    for panel in range(panels):
        for half in range(pivot_count // lanes):
            place = place_ref[panel : panel + 1, half * lanes : (half + 1) * lanes]
            owner = jnp.broadcast_to(lax.div(place, lanes), (group, lanes))
            lane = jnp.broadcast_to(place, (group, lanes)) - owner * lanes
            taken = jnp.zeros((group, lanes), jnp.float32)
            for d in range(device_count):
                taken = jnp.where(owner == d, jnp.take_along_axis(got_ref[d], lane, axis=1), taken)
            parts.append(taken)
    return jnp.concatenate(parts, axis=1)


def factor_kernel(
    device_count,
    place_ref,
    got_ref,
    points_ref,
    scales_ref,
    out_ref,
    res_ref,
    s_ref,
    right_ref,
    mean_ref,
    diag_ref,
    off_ref,
    x_ref,
    y_ref,
    inv_ref,
    weight_ref,
    z1_ref,
    z2_ref,
    feat_ref,
    k_top,
    k_low,
    c1_top,
    c1_low,
    c2_top,
    c2_low,
    square_ref,
    stage_ref,
    sems,
):
    panels, width = place_ref.shape
    row_count = points_ref.shape[1]
    total = panels * width
    windows = block // window
    tile = row_count // (2 * windows)
    scale = scale_column(scales_ref)

    scaled = gather_pivots(device_count, place_ref, got_ref) * scale
    left = narrow(features(scaled, True))
    right = narrow(features(scaled, False))
    right_ref[...] = right
    kernel = jnp.exp2(product(left, right, 0, 0))
    mean_ref[...] = jnp.broadcast_to(jnp.sum(kernel, axis=0, keepdims=True) * (1.0 / total), (group, total))
    s_ref[...] = jnp.where(iota((total, total), 0) == iota((total, total), 1), kernel + nugget, kernel)
    off_ref[1] = jnp.zeros((block, block), jnp.float32)

    def squares(new):
        parts = [new[:, q * lanes : (q + 1) * lanes] for q in range(width // lanes)]
        return tree_sum([p * p for p in parts])

    def first_task(rows):
        scaled = points_ref[:, rows] * scale
        left = narrow(features(scaled, True).T)
        feat_ref[rows, :] = left
        kernel = jnp.exp2(product(left, right_ref[:, : 2 * width])) - mean_ref[0:1, : 2 * width]
        k_top[rows, :], k_low[rows, :] = two_parts(kernel)

    def second_task(rows):
        top, low = k_top[rows, :width], k_low[rows, :width]
        a = jnp.concatenate([top, low, top], axis=1)
        new = product(a, weight_ref[...], 1, 1) + (shift_0)
        stage_ref[rows, :] = new
        square_ref[rows, :] = squares(new)
        kernel = widen(k_top[rows, width:]) + widen(k_low[rows, width:])
        c1_top[rows, :], c1_low[rows, :] = two_parts(kernel - product(a, z1_ref[...]) + shift_1)

    def third_task(rows):
        top, low = c1_top[rows, :], c1_low[rows, :]
        new = product(jnp.concatenate([top, low, top], axis=1), weight_ref[...], 1, 1)
        stage_ref[rows, :] = new
        square_ref[rows, :] = square_ref[rows, :] + squares(new)
        top, low = k_top[rows, :], k_low[rows, :]
        a = jnp.concatenate([top, low, top], axis=1)
        kernel = jnp.exp2(product(feat_ref[rows, :], right_ref[:, 2 * width :]))
        c2_top[rows, :], c2_low[rows, :] = two_parts(kernel - product(a, z2_ref[...]) - shift_2)

    def send(panel, rows):
        return pltpu.make_async_copy(
            stage_ref.at[rows, :],
            out_ref.at[rows, panel * width : (panel + 1) * width],
            sems.at[panel],
        )

    def span(at, size):
        return pl.ds(pl.multiple_of(at, size), size)

    at = lambda p: slice(p * width, (p + 1) * width)
    tasks = [first_task, second_task, third_task]
    for p in range(panels):
        one = slice(p * width, p * width + block)
        two = slice(p * width + block, (p + 1) * width)
        diag_ref[0] = s_ref[one, one]
        diag_ref[1] = s_ref[two, two]
        off_ref[0] = s_ref[one, two]

        @pl.loop(0, 2)
        def _(half, p=p):
            answer = []
            for w in factor_block(diag_ref[half], answer):
                tasks[p](span((half * windows + w) * tile, tile))
            x = jnp.concatenate(answer, axis=0)
            x_ref[half] = x
            y = product(x, off_ref[half], precision=high)
            y_ref[half] = y
            diag_ref[half + 1] = diag_ref[half + 1] - product(y, y, 0, 0, high)
            if p > 0:
                send(p - 1, span(half * (row_count // 2), row_count // 2)).start()

        if p > 0:
            send(p - 1, slice(0, row_count)).wait()
        x0, x1 = x_ref[0], x_ref[1]
        corner = product(x1, product(y_ref[0], x0, 0, 0, high), precision=high)
        inverse = jnp.concatenate(
            [
                jnp.concatenate([x0, jnp.zeros((block, block), jnp.float32)], axis=1),
                jnp.concatenate([-corner, x1], axis=1),
            ],
            axis=0,
        )
        top, low = two_parts(inverse)
        weight_ref[...] = jnp.concatenate([top, top, low], axis=1)
        if p == 0:
            inv_ref[...] = inverse
            shift_0 = product(mean_ref[:, at(0)], inverse, 1, 1, high)[0:1, :]
            y01 = product(inverse, s_ref[at(0), width:], precision=high)
            s_ref[at(1), width:] = s_ref[at(1), width:] - product(y01[:, :width], y01, 0, 0, high)
            s_ref[at(2), at(2)] = s_ref[at(2), at(2)] - product(y01[:, width:], y01[:, width:], 0, 0, high)
            z = product(inverse, y01[:, :width], 0, 0, high)
            top, low = two_parts(z)
            z1_ref[...] = jnp.concatenate([top, top, low], axis=0)
            shift_1 = (mean_ref[:, at(1)] - product(mean_ref[:, at(0)], z, precision=high))[0:1, :]
            s_ref[at(0), width:] = y01
        if p == 1:
            y12 = product(inverse, s_ref[at(1), at(2)], precision=high)
            s_ref[at(2), at(2)] = s_ref[at(2), at(2)] - product(y12, y12, 0, 0, high)
            zb = product(inverse, y12, 0, 0, high)
            rest = s_ref[at(0), at(2)] - product(s_ref[at(0), at(1)], zb, precision=high)
            z = jnp.concatenate([product(inv_ref[...], rest, 0, 0, high), zb], axis=0)
            top, low = two_parts(z)
            z2_ref[...] = jnp.concatenate([top, top, low], axis=0)
            shift_2 = product(mean_ref[:, : 2 * width], z, precision=high)[0:1, :]

    last = row_count // 8

    @pl.loop(0, row_count // last)
    def _(i):
        rows = span(i * last, last)
        top, low = c2_top[rows, :], c2_low[rows, :]
        new = product(jnp.concatenate([top, low, top], axis=1), weight_ref[...], 1, 1)
        stage_ref[rows, :] = new
        send(panels - 1, rows).start()
        total_square = square_ref[rows, :] + squares(new)
        res_ref[0:1, rows] = 1.0 - jnp.sum(total_square.T, axis=0, keepdims=True)

    send(panels - 1, slice(0, row_count)).wait()


def on_device(points, inv_scales, pivots):
    dim, row_count = points.shape
    panels, pivot_count = pivots.shape
    device_count = lax.axis_size("rows")
    slot_count = 4 * pivot_count // device_count
    total = panels * pivot_count
    assert dim == group and panels * slot_count <= lanes and panels == 3 and pivot_count == 2 * block
    f32, bf16 = jnp.float32, jnp.bfloat16
    shape = jax.ShapeDtypeStruct
    vmem = pl.BlockSpec(memory_space=pltpu.VMEM)
    smem = pl.BlockSpec(memory_space=pltpu.SMEM)

    send, place = pl.pallas_call(
        functools.partial(select_kernel, row_count, slot_count, device_count),
        out_shape=(shape((device_count, group, lanes), f32), shape((panels, pivot_count), jnp.int32)),
        in_specs=[vmem, vmem],
        out_specs=(vmem, vmem),
        compiler_params=pltpu.CompilerParams(vmem_limit_bytes=16 * 2**20),
        name="select",
    )(points, pivots)
    got = lax.all_to_all(send, "rows", 0, 0)
    width = pivot_count
    factor, residual = pl.pallas_call(
        functools.partial(factor_kernel, device_count),
        out_shape=(shape((row_count, total), f32), shape((1, row_count), f32)),
        in_specs=[vmem, vmem, vmem, smem],
        out_specs=(pl.BlockSpec(memory_space=pl.ANY), vmem),
        scratch_shapes=[
            pltpu.VMEM((total, total), f32),
            pltpu.VMEM((feature_rows, total), bf16),
            pltpu.VMEM((group, total), f32),
            pltpu.VMEM((3, block, block), f32),
            pltpu.VMEM((2, block, block), f32),
            pltpu.VMEM((2, block, block), f32),
            pltpu.VMEM((2, block, block), f32),
            pltpu.VMEM((width, width), f32),
            pltpu.VMEM((width, 3 * width), bf16),
            pltpu.VMEM((3 * width, width), bf16),
            pltpu.VMEM((6 * width, width), bf16),
            pltpu.VMEM((row_count, feature_rows), bf16),
            pltpu.VMEM((row_count, 2 * width), bf16),
            pltpu.VMEM((row_count, 2 * width), bf16),
            pltpu.VMEM((row_count, width), bf16),
            pltpu.VMEM((row_count, width), bf16),
            pltpu.VMEM((row_count, width), bf16),
            pltpu.VMEM((row_count, width), bf16),
            pltpu.VMEM((row_count, lanes), f32),
            pltpu.VMEM((row_count, width), f32),
            pltpu.SemaphoreType.DMA((panels,)),
        ],
        compiler_params=pltpu.CompilerParams(vmem_limit_bytes=60 * 2**20),
        name="factor",
    )(place, got, points, inv_scales)
    return factor, residual.reshape(row_count)


def solution(mesh):
    return jax.shard_map(
        on_device,
        mesh=mesh,
        in_specs=(P(None, "rows"), P(), P()),
        out_specs=(P("rows", None), P("rows")),
        check_vma=False,
    )
```

```python
import functools

import jax
import jax.numpy as jnp
from jax import lax
from jax.experimental import pallas as pl
from jax.experimental.pallas import tpu as pltpu
from jax.sharding import PartitionSpec as P

nugget = 0.1
exp2_scale = 1.2011224087864498
group = 8
lanes = 128
block = 128
window = 16
ahead = 1
last_tiles = 4
plan = (2, 2, 2, 2, 2, 2, 2, 0, 0, 0)
feature_rows = 64
high = lax.Precision.HIGHEST


def product(a, b, a_dim=1, b_dim=0, precision=None):
    return lax.dot_general(
        a,
        b,
        (((a_dim,), (b_dim,)), ((), ())),
        precision=precision,
        preferred_element_type=jnp.float32,
    )


def iota(shape, dim):
    return lax.broadcasted_iota(jnp.int32, shape, dim)


def widen(x):
    return x.astype(jnp.float32)


def narrow(x):
    return x.astype(jnp.bfloat16)


def select_kernel(
    row_count, slot_count, device_count, points_hbm, pivots_hbm, send_ref, place_ref, points_ref, pivots_ref, sems
):
    pivots_in = pltpu.make_async_copy(pivots_hbm, pivots_ref, sems.at[0])
    points_in = pltpu.make_async_copy(points_hbm, points_ref, sems.at[1])
    pivots_in.start()
    points_in.start()
    pivots_in.wait()
    panels, pivot_count = pivots_ref.shape
    me = lax.axis_index("rows")
    before = narrow(
        jnp.where(iota((pivot_count, pivot_count), 0) < iota((pivot_count, pivot_count), 1), 1.0, 0.0)
    )
    chosen_parts = []
    value_parts = []
    for panel in range(panels):
        index = pivots_ref[panel : panel + 1, :]
        owner = lax.div(index, row_count)
        local = index - owner * row_count
        owned = jnp.where(
            iota((device_count, pivot_count), 0) == jnp.broadcast_to(owner, (device_count, pivot_count)), 1.0, 0.0
        )
        counts = product(narrow(owned), before)
        rank = jnp.sum(owned * counts, axis=0, keepdims=True).astype(jnp.int32)
        slot = rank + panel * slot_count
        place_ref[panel : panel + 1, :] = owner * lanes + slot
        mine = jnp.where(owner == me, slot, -1)
        chosen_parts.append(
            jnp.where(iota((lanes, pivot_count), 0) == jnp.broadcast_to(mine, (lanes, pivot_count)), 1.0, 0.0)
        )
        tile = lax.div(local, lanes)
        lane = local - tile * lanes
        which = iota((group, pivot_count), 0)
        value_parts.append(
            jnp.where(which == 0, widen(tile), jnp.where(which == 1, widen(lane), 0.0))
        )
    chosen = narrow(jnp.concatenate(chosen_parts, axis=1))
    values = narrow(jnp.concatenate(value_parts, axis=1))
    found = product(values, chosen, 1, 1).astype(jnp.int32)
    tile = jnp.broadcast_to(found[0:1, :], (group, lanes))
    lane = jnp.broadcast_to(found[1:2, :], (group, lanes))
    points_in.wait()
    taken = jnp.zeros((group, lanes), jnp.float32)
    for t in range(row_count // lanes):
        here = jnp.take_along_axis(points_ref[:, t * lanes : (t + 1) * lanes], lane, axis=1)
        taken = jnp.where(tile == t, here, taken)
    for d in range(device_count):
        send_ref[d] = taken


def scale_column(scales_ref):
    sub = iota((group, 1), 0)
    column = jnp.zeros((group, 1), jnp.float32)
    for d in range(group):
        column = jnp.where(sub == d, scales_ref[d], column)
    return column * exp2_scale


def split3(x):
    top = widen(narrow(x))
    rest = x - top
    mid = widen(narrow(rest))
    return top, mid, widen(narrow(rest - mid))


def features(scaled, left):
    top, mid, low = split3(scaled)
    count = scaled.shape[1]
    norm = split3(jnp.broadcast_to(-0.5 * jnp.sum(scaled * scaled, axis=0, keepdims=True), (group, count)))
    sub = iota((group, count), 0)
    at = 0 if left else 3
    extra = jnp.where(sub < 6, 1.0, 0.0)
    for i in range(3):
        extra = jnp.where(sub == at + i, norm[i], extra)
    zero = jnp.zeros((group, count), jnp.float32)
    if left:
        parts = [top, top, mid, top, low, mid, extra, zero]
    else:
        parts = [top, mid, top, low, top, mid, extra, zero]
    return jnp.concatenate(parts, axis=0)


def spread(row, at):
    return jnp.broadcast_to(row[at : at + 1, :], row.shape)


def column(rows, at):
    return jnp.broadcast_to(rows[:, at : at + 1], rows.shape)


def tree_sum(terms):
    while len(terms) > 1:
        terms = [sum(terms[i : i + 2][1:], terms[i]) for i in range(0, len(terms), 2)]
    return terms[0]


def stack_left(x):
    top, mid, low = split3(x)
    return jnp.concatenate([top, top, mid, top, low, mid], axis=0)


def stack_right(x):
    top, mid, low = split3(x)
    return narrow(jnp.concatenate([top, mid, top, low, top, mid], axis=0))


def factor_block(matrix, answer):
    windows = block // window
    sub = iota((window, block), 0)
    lane = iota((window, block), 1)
    rows = [matrix[w * window : (w + 1) * window, :] for w in range(windows)]
    inv = [jnp.where(lane == sub + w * window, 1.0, 0.0) for w in range(windows)]
    for w in range(windows):
        first = w * window
        near = [column(rows[w], first + k) for k in range(window)]
        soon = range(w + 1, min(w + 1 + ahead, windows))
        after = [[column(rows[v], first + k) for k in range(window)] for v in soon]
        later = range(w + 1 + ahead, windows)
        if later:
            begin = later[0] * window // 16 * 16
            left = narrow(stack_left(rows[w])).T[begin:, :]
        row_s, row_x, forward = rows[w], inv[w], inv[w]
        diag = None
        for j in range(0, window, 2):
            a, b, c = spread(near[j], j), spread(near[j + 1], j), spread(near[j + 1], j + 1)
            recip = 1.0 / (a * c - b * b)
            n1 = near[j] - jnp.where(sub == j, 1.0, 0.0)
            n2 = near[j + 1] - jnp.where(sub == j + 1, 1.0, 0.0)
            m1 = (n1 * c - n2 * b) * recip
            m2 = (n2 * a - n1 * b) * recip
            for k in range(j + 2, window):
                near[k] = near[k] - (m1 * spread(near[k], j) + m2 * spread(near[k], j + 1))
            over = 1.0 / a
            f1 = jnp.where(sub > j, near[j] * over, 0.0)
            f2 = jnp.where(sub > j + 1, (near[j + 1] - near[j] * (b * over)) * (a * recip), 0.0)
            diag = a if diag is None else jnp.where(sub >= j, a, diag)
            diag = jnp.where(sub >= j + 1, c - b * (b * over), diag)
            row_s = row_s - (m1 * spread(row_s, j) + m2 * spread(row_s, j + 1))
            row_x = row_x - (m1 * spread(row_x, j) + m2 * spread(row_x, j + 1))
            forward = forward - f1 * spread(forward, j)
            if j + 2 < window:
                forward = forward - f2 * spread(forward, j + 1)
        answer.append(forward * lax.rsqrt(diag))
        for v, cols in zip(soon, after):
            rows[v] = rows[v] - tree_sum([cols[k] * spread(row_s, k) for k in range(window)])
            inv[v] = inv[v] - tree_sum([cols[k] * spread(row_x, k) for k in range(window)])
        if later:
            change = product(left, stack_right(jnp.concatenate([row_s, row_x], axis=1)))
            for v in later:
                at = v * window - begin
                rows[v] = rows[v] - change[at : at + window, :block]
                inv[v] = inv[v] - change[at : at + window, block:]
        yield w


def exact_product(a, b, a_dim=1, b_dim=0):
    top, mid, low = (narrow(part) for part in split3(a))
    if a_dim == 0:
        top, mid, low = top.T, mid.T, low.T
    left = jnp.concatenate([top, top, mid, top, low, mid], axis=1)
    top, mid, low = (narrow(part) for part in split3(b))
    return product(left, jnp.concatenate([top, mid, top, low, top, mid], axis=b_dim), 1, b_dim)


def two_parts(x):
    top = narrow(x)
    return top, narrow(x - widen(top))


def gather_pivots(device_count, place_ref, got_ref):
    panels, pivot_count = place_ref.shape
    parts = []
    for panel in range(panels):
        for half in range(pivot_count // lanes):
            place = place_ref[panel : panel + 1, half * lanes : (half + 1) * lanes]
            owner = jnp.broadcast_to(lax.div(place, lanes), (group, lanes))
            lane = jnp.broadcast_to(place, (group, lanes)) - owner * lanes
            taken = jnp.zeros((group, lanes), jnp.float32)
            for d in range(device_count):
                taken = jnp.where(owner == d, jnp.take_along_axis(got_ref[d], lane, axis=1), taken)
            parts.append(taken)
    return jnp.concatenate(parts, axis=1)


def factor_kernel(
    device_count,
    place_ref,
    got_ref,
    points_ref,
    scales_ref,
    out_ref,
    res_ref,
    s_ref,
    right_ref,
    mean_ref,
    diag_ref,
    off_ref,
    x_ref,
    y_ref,
    inv_ref,
    weight_ref,
    shift_ref,
    z1_ref,
    z2_ref,
    feat_ref,
    k_top,
    k_low,
    c1_top,
    c1_low,
    c2_top,
    c2_low,
    square_ref,
    stage_ref,
    sems,
):
    panels, width = place_ref.shape
    row_count = points_ref.shape[1]
    total = panels * width
    windows = block // window
    tile = row_count // 32
    scale = scale_column(scales_ref)

    scaled = gather_pivots(device_count, place_ref, got_ref) * scale
    left = narrow(features(scaled, True))
    right = narrow(features(scaled, False))
    right_ref[...] = right
    kernel = jnp.exp2(product(left, right, 0, 0))
    mean_ref[...] = jnp.broadcast_to(jnp.sum(kernel, axis=0, keepdims=True) * (1.0 / total), (group, total))
    s_ref[...] = jnp.where(iota((total, total), 0) == iota((total, total), 1), kernel + nugget, kernel)
    off_ref[1] = jnp.zeros((block, block), jnp.float32)

    def squares(new):
        parts = [new[:, q * lanes : (q + 1) * lanes] for q in range(width // lanes)]
        return tree_sum([p * p for p in parts])

    def first_task(rows):
        scaled = points_ref[:, rows] * scale
        left = narrow(features(scaled, True)).T
        feat_ref[rows, :] = left
        kernel = jnp.exp2(product(left, right_ref[:, : 2 * width])) - mean_ref[0:1, : 2 * width]
        k_top[rows, :], k_low[rows, :] = two_parts(kernel)

    def second_task(rows):
        top, low = k_top[rows, :width], k_low[rows, :width]
        a = jnp.concatenate([top, low, top], axis=1)
        new = product(a, weight_ref[0], 1, 1) + shift_ref[0, 0:1, :]
        stage_ref[rows, :] = new
        square_ref[rows, :] = squares(new)
        kernel = widen(k_top[rows, width:]) + widen(k_low[rows, width:])
        c1_top[rows, :], c1_low[rows, :] = two_parts(kernel - product(a, z1_ref[...]) + shift_ref[1, 0:1, :])

    def third_task(rows):
        top, low = c1_top[rows, :], c1_low[rows, :]
        new = product(jnp.concatenate([top, low, top], axis=1), weight_ref[1], 1, 1)
        stage_ref[rows, :] = new
        square_ref[rows, :] = square_ref[rows, :] + squares(new)
        top, low = k_top[rows, :], k_low[rows, :]
        a = jnp.concatenate([top, low, top], axis=1)
        kernel = jnp.exp2(product(feat_ref[rows, :], right_ref[:, 2 * width :]))
        c2_top[rows, :], c2_low[rows, :] = two_parts(kernel - product(a, z2_ref[...]) - shift_ref[2, 0:1, :])

    def last_task(rows):
        top, low = c2_top[rows, :], c2_low[rows, :]
        new = product(jnp.concatenate([top, low, top], axis=1), weight_ref[2], 1, 1)
        stage_ref[rows, :] = new
        total_square = square_ref[rows, :] + squares(new)
        res_ref[0:1, rows] = 1.0 - jnp.sum(total_square.T, axis=0, keepdims=True)

    def send(panel, part, rows):
        return pltpu.make_async_copy(
            stage_ref.at[rows, :],
            out_ref.at[rows, panel * width : (panel + 1) * width],
            sems.at[panel, part],
        )

    def span(at, size):
        return pl.ds(pl.multiple_of(at, tile), size)

    tiles = row_count // tile
    each = (tiles - last_tiles) // 2
    part_rows = [(0, each * tile), (each * tile, each * tile), (2 * each * tile, last_tiles * tile)]

    def wait(panel, part):
        send(panel, part, pl.ds(*part_rows[part])).wait()

    at = lambda p: slice(p * width, (p + 1) * width)
    tasks = [first_task, second_task, third_task]
    for p in range(panels):
        one = slice(p * width, p * width + block)
        two = slice(p * width + block, (p + 1) * width)
        diag_ref[0] = s_ref[one, one]
        diag_ref[1] = s_ref[two, two]
        off_ref[0] = s_ref[one, two]

        @pl.loop(0, 2)
        def _(half, p=p):
            given = []

            def work(count):
                for _ in range(count):
                    tasks[p](span((half * each + len(given)) * tile, tile))
                    given.append(0)

            answer = []
            for w in factor_block(diag_ref[half], answer):
                work(plan[w])
            x = jnp.concatenate(answer, axis=0)
            x_ref[half] = x
            y = exact_product(x, off_ref[half])
            work(plan[windows])
            y_ref[half] = y
            diag_ref[half + 1] = diag_ref[half + 1] - exact_product(y, y, 0, 0)
            work(plan[windows + 1])
            assert len(given) == each
            if p > 0:
                send(p - 1, half, span(half * (each * tile), each * tile)).start()

        rest = [functools.partial(tasks[p], pl.ds((2 * each + i) * tile, tile)) for i in range(last_tiles)]
        x0, x1 = x_ref[0], x_ref[1]
        corner = exact_product(x1, exact_product(y_ref[0], x0, 0, 0))
        if p > 1:
            wait(p - 2, 2)
        rest.pop(0)()
        inverse = jnp.concatenate(
            [
                jnp.concatenate([x0, jnp.zeros((block, block), jnp.float32)], axis=1),
                jnp.concatenate([-corner, x1], axis=1),
            ],
            axis=0,
        )
        top, low = two_parts(inverse)
        weight_ref[p] = jnp.concatenate([top, top, low], axis=1)
        if p == 0:
            inv_ref[...] = inverse
            shift_ref[0] = product(mean_ref[:, at(0)], inverse, 1, 1, high)
            y01 = exact_product(inverse, s_ref[at(0), width:])
            rest.pop(0)()
            s_ref[at(1), width:] = s_ref[at(1), width:] - exact_product(y01[:, :width], y01, 0, 0)
            s_ref[at(2), at(2)] = s_ref[at(2), at(2)] - exact_product(y01[:, width:], y01[:, width:], 0, 0)
            z = exact_product(inverse, y01[:, :width], 0, 0)
            top, low = two_parts(z)
            z1_ref[...] = jnp.concatenate([top, top, low], axis=0)
            shift_ref[1] = mean_ref[:, at(1)] - product(mean_ref[:, at(0)], z, precision=high)
            s_ref[at(0), width:] = y01
        if p == 1:
            y12 = exact_product(inverse, s_ref[at(1), at(2)])
            rest.pop(0)()
            s_ref[at(2), at(2)] = s_ref[at(2), at(2)] - exact_product(y12, y12, 0, 0)
            zb = exact_product(inverse, y12, 0, 0)
            far = s_ref[at(0), at(2)] - exact_product(s_ref[at(0), at(1)], zb)
            z = jnp.concatenate([exact_product(inv_ref[...], far, 0, 0), zb], axis=0)
            top, low = two_parts(z)
            z2_ref[...] = jnp.concatenate([top, top, low], axis=0)
            shift_ref[2] = product(mean_ref[:, : 2 * width], z, precision=high)
        for task in rest:
            task()
        if p == 1:
            wait(0, 0)
            wait(0, 1)
        if p > 0:
            send(p - 1, 2, pl.ds(*part_rows[2])).start()

    pending = []
    for part, (start, size) in enumerate(part_rows):
        wait(panels - 2, part)
        done = start
        while done < start + size:
            now = min(2 * tile, start + size - done)
            last_task(pl.ds(done, now))
            pending.append(send(panels - 1, part, pl.ds(done, now)))
            done += now
            if len(pending) > 2:
                pending.pop(0).start()
    for copy in pending:
        copy.start()
    for part in range(3):
        wait(panels - 1, part)


def on_device(points, inv_scales, pivots):
    dim, row_count = points.shape
    panels, pivot_count = pivots.shape
    device_count = lax.axis_size("rows")
    slot_count = 4 * pivot_count // device_count
    total = panels * pivot_count
    assert dim == group and panels * slot_count <= lanes and panels == 3 and pivot_count == 2 * block
    f32, bf16 = jnp.float32, jnp.bfloat16
    shape = jax.ShapeDtypeStruct
    vmem = pl.BlockSpec(memory_space=pltpu.VMEM)
    smem = pl.BlockSpec(memory_space=pltpu.SMEM)
    anywhere = pl.BlockSpec(memory_space=pltpu.HBM)

    send, place = pl.pallas_call(
        functools.partial(select_kernel, row_count, slot_count, device_count),
        out_shape=(shape((device_count, group, lanes), f32), shape((panels, pivot_count), jnp.int32)),
        in_specs=[anywhere, anywhere],
        out_specs=(vmem, vmem),
        scratch_shapes=[
            pltpu.VMEM((dim, row_count), f32),
            pltpu.VMEM((panels, pivot_count), jnp.int32),
            pltpu.SemaphoreType.DMA((2,)),
        ],
        compiler_params=pltpu.CompilerParams(vmem_limit_bytes=16 * 2**20),
        name="select",
    )(points, pivots)
    got = lax.all_to_all(send, "rows", 0, 0)
    width = pivot_count
    factor, residual = pl.pallas_call(
        functools.partial(factor_kernel, device_count),
        out_shape=(shape((row_count, total), f32), shape((1, row_count), f32)),
        in_specs=[vmem, vmem, vmem, smem],
        out_specs=(pl.BlockSpec(memory_space=pl.ANY), vmem),
        scratch_shapes=[
            pltpu.VMEM((total, total), f32),
            pltpu.VMEM((feature_rows, total), bf16),
            pltpu.VMEM((group, total), f32),
            pltpu.VMEM((3, block, block), f32),
            pltpu.VMEM((2, block, block), f32),
            pltpu.VMEM((2, block, block), f32),
            pltpu.VMEM((2, block, block), f32),
            pltpu.VMEM((width, width), f32),
            pltpu.VMEM((panels, width, 3 * width), bf16),
            pltpu.VMEM((panels, group, width), f32),
            pltpu.VMEM((3 * width, width), bf16),
            pltpu.VMEM((6 * width, width), bf16),
            pltpu.VMEM((row_count, feature_rows), bf16),
            pltpu.VMEM((row_count, 2 * width), bf16),
            pltpu.VMEM((row_count, 2 * width), bf16),
            pltpu.VMEM((row_count, width), bf16),
            pltpu.VMEM((row_count, width), bf16),
            pltpu.VMEM((row_count, width), bf16),
            pltpu.VMEM((row_count, width), bf16),
            pltpu.VMEM((row_count, lanes), f32),
            pltpu.VMEM((row_count, width), f32),
            pltpu.SemaphoreType.DMA((panels, 3)),
        ],
        compiler_params=pltpu.CompilerParams(vmem_limit_bytes=60 * 2**20),
        name="factor",
    )(place, got, points, inv_scales)
    return factor, residual.reshape(row_count)


def solution(mesh):
    return jax.shard_map(
        on_device,
        mesh=mesh,
        in_specs=(P(None, "rows"), P(), P()),
        out_specs=(P("rows", None), P("rows")),
        check_vma=False,
    )
```

```python
import functools

import jax
import jax.numpy as jnp
from jax import lax
from jax.experimental import pallas as pl
from jax.experimental.pallas import tpu as pltpu
from jax.sharding import PartitionSpec as P

nugget = 0.1
exp2_scale = 1.2011224087864498
group = 8
lanes = 128
block = 128
window = 16
ahead = 1
last_tiles = 8
plan = (2, 2, 2, 2, 2, 1, 1, 0, 0, 0)
feature_rows = 64
high = lax.Precision.HIGHEST


def product(a, b, a_dim=1, b_dim=0, precision=None):
    return lax.dot_general(
        a,
        b,
        (((a_dim,), (b_dim,)), ((), ())),
        precision=precision,
        preferred_element_type=jnp.float32,
    )


def iota(shape, dim):
    return lax.broadcasted_iota(jnp.int32, shape, dim)


def widen(x):
    return x.astype(jnp.float32)


def narrow(x):
    return x.astype(jnp.bfloat16)


def select_kernel(
    row_count, slot_count, device_count, points_hbm, pivots_hbm, send_ref, place_ref, points_ref, pivots_ref, sems
):
    pivots_in = pltpu.make_async_copy(pivots_hbm, pivots_ref, sems.at[0])
    points_in = pltpu.make_async_copy(points_hbm, points_ref, sems.at[1])
    pivots_in.start()
    points_in.start()
    pivots_in.wait()
    panels, pivot_count = pivots_ref.shape
    me = lax.axis_index("rows")
    before = narrow(
        jnp.where(iota((pivot_count, pivot_count), 0) < iota((pivot_count, pivot_count), 1), 1.0, 0.0)
    )
    chosen_parts = []
    value_parts = []
    for panel in range(panels):
        index = pivots_ref[panel : panel + 1, :]
        owner = lax.div(index, row_count)
        local = index - owner * row_count
        owned = jnp.where(
            iota((device_count, pivot_count), 0) == jnp.broadcast_to(owner, (device_count, pivot_count)), 1.0, 0.0
        )
        counts = product(narrow(owned), before)
        rank = jnp.sum(owned * counts, axis=0, keepdims=True).astype(jnp.int32)
        slot = rank + panel * slot_count
        place_ref[panel : panel + 1, :] = owner * lanes + slot
        mine = jnp.where(owner == me, slot, -1)
        chosen_parts.append(
            jnp.where(iota((lanes, pivot_count), 0) == jnp.broadcast_to(mine, (lanes, pivot_count)), 1.0, 0.0)
        )
        tile = lax.div(local, lanes)
        lane = local - tile * lanes
        which = iota((group, pivot_count), 0)
        value_parts.append(
            jnp.where(which == 0, widen(tile), jnp.where(which == 1, widen(lane), 0.0))
        )
    chosen = narrow(jnp.concatenate(chosen_parts, axis=1))
    values = narrow(jnp.concatenate(value_parts, axis=1))
    found = product(values, chosen, 1, 1).astype(jnp.int32)
    tile = jnp.broadcast_to(found[0:1, :], (group, lanes))
    lane = jnp.broadcast_to(found[1:2, :], (group, lanes))
    points_in.wait()
    taken = jnp.zeros((group, lanes), jnp.float32)
    for t in range(row_count // lanes):
        here = jnp.take_along_axis(points_ref[:, t * lanes : (t + 1) * lanes], lane, axis=1)
        taken = jnp.where(tile == t, here, taken)
    for d in range(device_count):
        send_ref[d] = taken


def scale_column(scales_ref):
    sub = iota((group, 1), 0)
    column = jnp.zeros((group, 1), jnp.float32)
    for d in range(group):
        column = jnp.where(sub == d, scales_ref[d], column)
    return column * exp2_scale


def split3(x):
    top = widen(narrow(x))
    rest = x - top
    mid = widen(narrow(rest))
    return top, mid, widen(narrow(rest - mid))


def features(scaled, left):
    top, mid, low = split3(scaled)
    count = scaled.shape[1]
    norm = split3(jnp.broadcast_to(-0.5 * jnp.sum(scaled * scaled, axis=0, keepdims=True), (group, count)))
    sub = iota((group, count), 0)
    at = 0 if left else 3
    extra = jnp.where(sub < 6, 1.0, 0.0)
    for i in range(3):
        extra = jnp.where(sub == at + i, norm[i], extra)
    zero = jnp.zeros((group, count), jnp.float32)
    if left:
        parts = [top, top, mid, top, low, mid, extra, zero]
    else:
        parts = [top, mid, top, low, top, mid, extra, zero]
    return jnp.concatenate(parts, axis=0)


def spread(row, at):
    return jnp.broadcast_to(row[at : at + 1, :], row.shape)


def column(rows, at):
    return jnp.broadcast_to(rows[:, at : at + 1], rows.shape)


def tree_sum(terms):
    while len(terms) > 1:
        terms = [sum(terms[i : i + 2][1:], terms[i]) for i in range(0, len(terms), 2)]
    return terms[0]


def stack_left(x):
    top, mid, low = split3(x)
    return jnp.concatenate([top, top, mid, top, low, mid], axis=0)


def stack_right(x):
    top, mid, low = split3(x)
    return narrow(jnp.concatenate([top, mid, top, low, top, mid], axis=0))


def factor_block(matrix, answer):
    windows = block // window
    sub = iota((window, block), 0)
    lane = iota((window, block), 1)
    rows = [matrix[w * window : (w + 1) * window, :] for w in range(windows)]
    inv = [jnp.where(lane == sub + w * window, 1.0, 0.0) for w in range(windows)]
    for w in range(windows):
        first = w * window
        near = [column(rows[w], first + k) for k in range(window)]
        soon = range(w + 1, min(w + 1 + ahead, windows))
        after = [[column(rows[v], first + k) for k in range(window)] for v in soon]
        later = range(w + 1 + ahead, windows)
        if later:
            begin = later[0] * window // 16 * 16
            left = narrow(stack_left(rows[w])).T[begin:, :]
        row_s, row_x, forward = rows[w], inv[w], inv[w]
        diag = None
        for j in range(0, window, 2):
            a, b, c = spread(near[j], j), spread(near[j + 1], j), spread(near[j + 1], j + 1)
            recip = 1.0 / (a * c - b * b)
            n1 = near[j] - jnp.where(sub == j, 1.0, 0.0)
            n2 = near[j + 1] - jnp.where(sub == j + 1, 1.0, 0.0)
            m1 = (n1 * c - n2 * b) * recip
            m2 = (n2 * a - n1 * b) * recip
            for k in range(j + 2, window):
                near[k] = near[k] - (m1 * spread(near[k], j) + m2 * spread(near[k], j + 1))
            over = 1.0 / a
            f1 = jnp.where(sub > j, near[j] * over, 0.0)
            f2 = jnp.where(sub > j + 1, (near[j + 1] - near[j] * (b * over)) * (a * recip), 0.0)
            diag = a if diag is None else jnp.where(sub >= j, a, diag)
            diag = jnp.where(sub >= j + 1, c - b * (b * over), diag)
            row_s = row_s - (m1 * spread(row_s, j) + m2 * spread(row_s, j + 1))
            row_x = row_x - (m1 * spread(row_x, j) + m2 * spread(row_x, j + 1))
            forward = forward - f1 * spread(forward, j)
            if j + 2 < window:
                forward = forward - f2 * spread(forward, j + 1)
        answer.append(forward * lax.rsqrt(diag))
        for v, cols in zip(soon, after):
            rows[v] = rows[v] - tree_sum([cols[k] * spread(row_s, k) for k in range(window)])
            inv[v] = inv[v] - tree_sum([cols[k] * spread(row_x, k) for k in range(window)])
        if later:
            change = product(left, stack_right(jnp.concatenate([row_s, row_x], axis=1)))
            for v in later:
                at = v * window - begin
                rows[v] = rows[v] - change[at : at + window, :block]
                inv[v] = inv[v] - change[at : at + window, block:]
        yield w


def exact_product(a, b, a_dim=1, b_dim=0):
    top, mid, low = (narrow(part) for part in split3(a))
    if a_dim == 0:
        top, mid, low = top.T, mid.T, low.T
    left = jnp.concatenate([top, top, mid, top, low, mid], axis=1)
    top, mid, low = (narrow(part) for part in split3(b))
    return product(left, jnp.concatenate([top, mid, top, low, top, mid], axis=b_dim), 1, b_dim)


def two_parts(x):
    top = narrow(x)
    return top, narrow(x - widen(top))


def gather_pivots(device_count, place_ref, got_ref):
    panels, pivot_count = place_ref.shape
    parts = []
    for panel in range(panels):
        for half in range(pivot_count // lanes):
            place = place_ref[panel : panel + 1, half * lanes : (half + 1) * lanes]
            owner = jnp.broadcast_to(lax.div(place, lanes), (group, lanes))
            lane = jnp.broadcast_to(place, (group, lanes)) - owner * lanes
            taken = jnp.zeros((group, lanes), jnp.float32)
            for d in range(device_count):
                taken = jnp.where(owner == d, jnp.take_along_axis(got_ref[d], lane, axis=1), taken)
            parts.append(taken)
    return jnp.concatenate(parts, axis=1)


def factor_kernel(
    device_count,
    place_ref,
    got_ref,
    points_ref,
    scales_ref,
    out_ref,
    res_ref,
    s_ref,
    right_ref,
    mean_ref,
    diag_ref,
    off_ref,
    x_ref,
    y_ref,
    inv_ref,
    weight_ref,
    shift_ref,
    z1_ref,
    z2_ref,
    feat_ref,
    k_top,
    k_low,
    c1_top,
    c1_low,
    c2_top,
    c2_low,
    square_ref,
    stage_ref,
    sems,
):
    panels, width = place_ref.shape
    row_count = points_ref.shape[1]
    total = panels * width
    windows = block // window
    tile = row_count // 32
    scale = scale_column(scales_ref)

    scaled = gather_pivots(device_count, place_ref, got_ref) * scale
    left = narrow(features(scaled, True))
    right = narrow(features(scaled, False))
    right_ref[...] = right
    kernel = jnp.exp2(product(left, right, 0, 0))
    mean_ref[...] = jnp.broadcast_to(jnp.sum(kernel, axis=0, keepdims=True) * (1.0 / total), (group, total))
    s_ref[...] = jnp.where(iota((total, total), 0) == iota((total, total), 1), kernel + nugget, kernel)
    off_ref[1] = jnp.zeros((block, block), jnp.float32)

    def squares(new):
        parts = [new[:, q * lanes : (q + 1) * lanes] for q in range(width // lanes)]
        return tree_sum([p * p for p in parts])

    def first_task(rows):
        scaled = points_ref[:, rows] * scale
        left = narrow(features(scaled, True)).T
        feat_ref[rows, :] = left
        kernel = jnp.exp2(product(left, right_ref[:, : 2 * width])) - mean_ref[0:1, : 2 * width]
        k_top[rows, :], k_low[rows, :] = two_parts(kernel)

    def second_task(rows):
        top, low = k_top[rows, :width], k_low[rows, :width]
        a = jnp.concatenate([top, low, top], axis=1)
        new = product(a, weight_ref[0], 1, 1) + shift_ref[0, 0:1, :]
        stage_ref[rows, :] = new
        square_ref[rows, :] = squares(new)
        kernel = widen(k_top[rows, width:]) + widen(k_low[rows, width:])
        c1_top[rows, :], c1_low[rows, :] = two_parts(kernel - product(a, z1_ref[...]) + shift_ref[1, 0:1, :])

    def third_task(rows):
        top, low = c1_top[rows, :], c1_low[rows, :]
        new = product(jnp.concatenate([top, low, top], axis=1), weight_ref[1], 1, 1)
        stage_ref[rows, :] = new
        square_ref[rows, :] = square_ref[rows, :] + squares(new)
        top, low = k_top[rows, :], k_low[rows, :]
        a = jnp.concatenate([top, low, top], axis=1)
        kernel = jnp.exp2(product(feat_ref[rows, :], right_ref[:, 2 * width :]))
        c2_top[rows, :], c2_low[rows, :] = two_parts(kernel - product(a, z2_ref[...]) - shift_ref[2, 0:1, :])

    def last_task(rows):
        top, low = c2_top[rows, :], c2_low[rows, :]
        new = product(jnp.concatenate([top, low, top], axis=1), weight_ref[2], 1, 1)
        stage_ref[rows, :] = new
        total_square = square_ref[rows, :] + squares(new)
        res_ref[0:1, rows] = 1.0 - jnp.sum(total_square.T, axis=0, keepdims=True)

    def send(panel, part, rows):
        return pltpu.make_async_copy(
            stage_ref.at[rows, :],
            out_ref.at[rows, panel * width : (panel + 1) * width],
            sems.at[panel, part],
        )

    def span(at, size):
        return pl.ds(pl.multiple_of(at, tile), size)

    tiles = row_count // tile
    each = (tiles - last_tiles) // 2
    part_rows = [(0, each * tile), (each * tile, each * tile), (2 * each * tile, last_tiles * tile)]

    def wait(panel, part):
        send(panel, part, pl.ds(*part_rows[part])).wait()

    at = lambda p: slice(p * width, (p + 1) * width)
    tasks = [first_task, second_task, third_task]
    for p in range(panels):
        one = slice(p * width, p * width + block)
        two = slice(p * width + block, (p + 1) * width)
        diag_ref[0] = s_ref[one, one]
        diag_ref[1] = s_ref[two, two]
        off_ref[0] = s_ref[one, two]

        @pl.loop(0, 2)
        def _(half, p=p):
            given = []

            def work(count):
                for _ in range(count):
                    tasks[p](span((half * each + len(given)) * tile, tile))
                    given.append(0)

            answer = []
            for w in factor_block(diag_ref[half], answer):
                work(plan[w])
            x = jnp.concatenate(answer, axis=0)
            x_ref[half] = x
            y = exact_product(x, off_ref[half])
            work(plan[windows])
            y_ref[half] = y
            diag_ref[half + 1] = diag_ref[half + 1] - exact_product(y, y, 0, 0)
            work(plan[windows + 1])
            assert len(given) == each
            if p > 0:
                send(p - 1, half, span(half * (each * tile), each * tile)).start()

        rest = [functools.partial(tasks[p], pl.ds((2 * each + i) * tile, tile)) for i in range(last_tiles)]
        x0, x1 = x_ref[0], x_ref[1]
        corner = exact_product(x1, exact_product(y_ref[0], x0, 0, 0))
        if p > 1:
            wait(p - 2, 2)
        rest.pop(0)()
        rest.pop(0)()
        inverse = jnp.concatenate(
            [
                jnp.concatenate([x0, jnp.zeros((block, block), jnp.float32)], axis=1),
                jnp.concatenate([-corner, x1], axis=1),
            ],
            axis=0,
        )
        top, low = two_parts(inverse)
        weight_ref[p] = jnp.concatenate([top, top, low], axis=1)
        if p == 0:
            inv_ref[...] = inverse
            shift_ref[0] = product(mean_ref[:, at(0)], inverse, 1, 1, high)
            y01 = exact_product(inverse, s_ref[at(0), width:])
            rest.pop(0)()
            rest.pop(0)()
            s_ref[at(1), width:] = s_ref[at(1), width:] - exact_product(y01[:, :width], y01, 0, 0)
            s_ref[at(2), at(2)] = s_ref[at(2), at(2)] - exact_product(y01[:, width:], y01[:, width:], 0, 0)
            rest.pop(0)()
            rest.pop(0)()
            z = exact_product(inverse, y01[:, :width], 0, 0)
            top, low = two_parts(z)
            z1_ref[...] = jnp.concatenate([top, top, low], axis=0)
            shift_ref[1] = mean_ref[:, at(1)] - product(mean_ref[:, at(0)], z, precision=high)
            s_ref[at(0), width:] = y01
        if p == 1:
            y12 = exact_product(inverse, s_ref[at(1), at(2)])
            rest.pop(0)()
            rest.pop(0)()
            s_ref[at(2), at(2)] = s_ref[at(2), at(2)] - exact_product(y12, y12, 0, 0)
            zb = exact_product(inverse, y12, 0, 0)
            rest.pop(0)()
            rest.pop(0)()
            far = s_ref[at(0), at(2)] - exact_product(s_ref[at(0), at(1)], zb)
            z = jnp.concatenate([exact_product(inv_ref[...], far, 0, 0), zb], axis=0)
            top, low = two_parts(z)
            z2_ref[...] = jnp.concatenate([top, top, low], axis=0)
            shift_ref[2] = product(mean_ref[:, : 2 * width], z, precision=high)
        for task in rest:
            task()
        if p == 1:
            wait(0, 0)
            wait(0, 1)
        if p > 0:
            send(p - 1, 2, pl.ds(*part_rows[2])).start()

    pending = []
    for part, (start, size) in enumerate(part_rows):
        wait(panels - 2, part)
        done = start
        while done < start + size:
            now = min(2 * tile, start + size - done)
            last_task(pl.ds(done, now))
            pending.append(send(panels - 1, part, pl.ds(done, now)))
            done += now
            if len(pending) > 2:
                pending.pop(0).start()
    for copy in pending:
        copy.start()
    for part in range(3):
        wait(panels - 1, part)


def on_device(points, inv_scales, pivots):
    dim, row_count = points.shape
    panels, pivot_count = pivots.shape
    device_count = lax.axis_size("rows")
    slot_count = 4 * pivot_count // device_count
    total = panels * pivot_count
    assert dim == group and panels * slot_count <= lanes and panels == 3 and pivot_count == 2 * block
    f32, bf16 = jnp.float32, jnp.bfloat16
    shape = jax.ShapeDtypeStruct
    vmem = pl.BlockSpec(memory_space=pltpu.VMEM)
    smem = pl.BlockSpec(memory_space=pltpu.SMEM)
    anywhere = pl.BlockSpec(memory_space=pltpu.HBM)

    send, place = pl.pallas_call(
        functools.partial(select_kernel, row_count, slot_count, device_count),
        out_shape=(shape((device_count, group, lanes), f32), shape((panels, pivot_count), jnp.int32)),
        in_specs=[anywhere, anywhere],
        out_specs=(vmem, vmem),
        scratch_shapes=[
            pltpu.VMEM((dim, row_count), f32),
            pltpu.VMEM((panels, pivot_count), jnp.int32),
            pltpu.SemaphoreType.DMA((2,)),
        ],
        compiler_params=pltpu.CompilerParams(vmem_limit_bytes=60 * 2**20),
        name="select",
    )(points, pivots)
    got = lax.all_to_all(send, "rows", 0, 0)
    width = pivot_count
    factor, residual = pl.pallas_call(
        functools.partial(factor_kernel, device_count),
        out_shape=(shape((row_count, total), f32), shape((1, row_count), f32)),
        in_specs=[vmem, vmem, vmem, smem],
        out_specs=(pl.BlockSpec(memory_space=pl.ANY), vmem),
        scratch_shapes=[
            pltpu.VMEM((total, total), f32),
            pltpu.VMEM((feature_rows, total), bf16),
            pltpu.VMEM((group, total), f32),
            pltpu.VMEM((3, block, block), f32),
            pltpu.VMEM((2, block, block), f32),
            pltpu.VMEM((2, block, block), f32),
            pltpu.VMEM((2, block, block), f32),
            pltpu.VMEM((width, width), f32),
            pltpu.VMEM((panels, width, 3 * width), bf16),
            pltpu.VMEM((panels, group, width), f32),
            pltpu.VMEM((3 * width, width), bf16),
            pltpu.VMEM((6 * width, width), bf16),
            pltpu.VMEM((row_count, feature_rows), bf16),
            pltpu.VMEM((row_count, 2 * width), bf16),
            pltpu.VMEM((row_count, 2 * width), bf16),
            pltpu.VMEM((row_count, width), bf16),
            pltpu.VMEM((row_count, width), bf16),
            pltpu.VMEM((row_count, width), bf16),
            pltpu.VMEM((row_count, width), bf16),
            pltpu.VMEM((row_count, lanes), f32),
            pltpu.VMEM((row_count, width), f32),
            pltpu.SemaphoreType.DMA((panels, 3)),
        ],
        compiler_params=pltpu.CompilerParams(vmem_limit_bytes=60 * 2**20),
        name="factor",
    )(place, got, points, inv_scales)
    return factor, residual.reshape(row_count)


def solution(mesh):
    return jax.shard_map(
        on_device,
        mesh=mesh,
        in_specs=(P(None, "rows"), P(), P()),
        out_specs=(P("rows", None), P("rows")),
        check_vma=False,
    )
```
